512 devices in a mesh: frame: 64 (over x, z), uly: 8 (over y, core).
Axes of the slice: x: 4, y: 4, z: 16, core: 2. Of those that a mesh axis runs over, the one named last changes fastest.
Arguments:
- queries: bfloat16 [65536, 3072], P(('frame', 'uly')), may hold values from -7.5 to 7.5
- keys: bfloat16 [65536, 3072], P(('frame', 'uly')), may hold values from -7.5 to 7.5
- values: bfloat16 [65536, 3072], P(('frame', 'uly')), may hold values from -6 to 6
- text_k: bfloat16 [4, 128, 3072], P(None, 'frame', 'uly'), may hold values from -7.5 to 7.5
- text_v: bfloat16 [4, 128, 3072], P(None, 'frame', 'uly'), may hold values from -6 to 6
- text_len: int32 [4], replicated, may hold values from 1 to 128, 256 in all
- seg_frames: int32 [4], replicated, may hold values from 1 to 512, 1024 in all
Outputs:
- grad_queries: bfloat16 [65536, 3072], P(('frame', 'uly'))
- grad_keys: bfloat16 [65536, 3072], P(('frame', 'uly'))
- grad_values: bfloat16 [65536, 3072], P(('frame', 'uly'))
- grad_text_k: float32 [4, 128, 3072], P(None, 'frame', 'uly')
- grad_text_v: float32 [4, 128, 3072], P(None, 'frame', 'uly')
The draws below stay inside these ranges and needn't reach their ends.
Inputs may be any that keep to these rules, and one draw needn't show every extreme that they name: `text_len`: the entries sum to 256. `seg_frames`: the segments cover the 1024 frames in order and sum to 1024.
All inputs are finite; a program needn't handle non-finite values.
Results may differ from the reference program's by a relative error of at most 0.015.
Values may be sent and summed in bfloat16 or wider, within the bound.
A program may use at most 128 MiB of HBM per device.

```python
import math
import jax
import jax.numpy as jnp
import numpy as np
from jax import lax

HEADS = 24
HD = 128
FT = 64
TXT = 128
NSEG = 4
FRAMES = 1024
TOKENS = 65536


def rough_field(key, shape):
    return jnp.clip(1.5 * jax.random.normal(key, shape, jnp.float32), -7.5, 7.5)


def draw_queries(key, part):
    key = jax.random.fold_in(key, 1)
    field = rough_field(key, (TOKENS, HEADS * HD))
    return field.astype(jnp.bfloat16)


def draw_keys(key, part):
    key = jax.random.fold_in(key, 2)
    field = rough_field(key, (TOKENS, HEADS * HD))
    return field.astype(jnp.bfloat16)


def draw_text_k(key, part):
    key = jax.random.fold_in(key, 3)
    field = rough_field(key, (NSEG, TXT, HEADS * HD))
    return field.astype(jnp.bfloat16)


def steps_of(key, extent, shards, smallest, high):
    def one(axis_at, blocks):
        steps = jax.random.uniform(jax.random.fold_in(jax.random.fold_in(key, 6), axis_at), (blocks,), jnp.float32, smallest / len(shards), high / len(shards))
        return jnp.repeat(jnp.exp(steps), extent[axis_at] // blocks).reshape((-1,) + (1,) * (len(extent) - axis_at - 1))

    level = one(*shards[0])
    for cut in shards[1:]:
        level = level * one(*cut)
    return level


def profile(count, total, limit, slope):
    portions = [(1 << 20) // math.isqrt(rank ** slope) + 1 for rank in range(2, count + 1)]
    spare, given = total - limit - (count - 1), [1] * (count - 1)
    while spare > 0:
        candidates = [i for i in range(count - 1) if given[i] < limit]
        pool, budget = sum([portions[i] for i in candidates]), spare
        for i in candidates:
            more = min(limit - given[i], max(1, budget * portions[i] // pool), spare)
            given[i] = given[i] + more
            spare = spare - more
    return np.array([limit] + given)


def uneven(key, number_of, total, limit, skew):
    if number_of == 2:
        one = jax.random.randint(key, (), max(1, total - limit), min(limit, total - 1) + 1)
        return jnp.stack([one, total - one])
    tallies = jnp.asarray(profile(number_of, total, limit, skew), jnp.int32)
    pairs = (number_of - 1) // 2
    source_of, sink = tallies[1:1 + 2 * pairs:2], tallies[2:2 + 2 * pairs:2]
    slack = jnp.minimum(source_of - 1, limit - sink)
    shifted = jax.random.randint(jax.random.fold_in(key, 1), (pairs,), 0, 1 << 20) % (slack + 1)
    tallies = tallies.at[1:1 + 2 * pairs:2].set(source_of - shifted).at[2:2 + 2 * pairs:2].set(sink + shifted)
    return tallies[jax.random.permutation(jax.random.fold_in(key, 2), number_of)]


def bell_draw(stream_key, shape, scale, most, split=(), kind=jnp.bfloat16):
    result = jax.random.normal(stream_key, shape, jnp.float32) * scale
    if len(split) > 0:
        result = steps_of(stream_key, shape, split, -0.22, 0.18) * result
    return jnp.clip(result, min=-most, max=most).astype(kind)


def setup_inputs(seed: int = 0) -> dict:
    key_of = jax.random.split(jax.random.key(seed), 8)
    return {
        "queries": draw_queries(jax.random.fold_in(key_of[7], 71), 0),
        "keys": draw_keys(jax.random.fold_in(key_of[7], 71), 0),
        "values": bell_draw(key_of[2], (TOKENS, HEADS * HD), 1.0, 6.0, ((0, 512),)),
        "text_k": draw_text_k(jax.random.fold_in(key_of[7], 71), 0),
        "text_v": bell_draw(key_of[4], (NSEG, TXT, HEADS * HD), 1.0, 6.0, ((1, 64), (2, 8))),
        "text_len": uneven(key_of[5], NSEG, 2 * TXT, TXT, 2).astype(jnp.int32),
        "seg_frames": uneven(key_of[6], NSEG, FRAMES, FRAMES // 2, 1).astype(jnp.int32),
    }


def normalize(scores):
    top = jnp.max(scores, axis=-1, keepdims=True)
    lse = top + jnp.log(jnp.sum(jnp.exp(scores - top), axis=-1, keepdims=True))
    return jnp.exp(scores - lse), lse


def keep_bf16(array):
    return lax.optimization_barrier(array.astype(jnp.bfloat16)).astype(jnp.float32)


def reference(queries, keys, values, text_k, text_v, text_len, seg_frames):
    scale = HD ** -0.5
    shape4 = (FRAMES, FT, HEADS, HD)
    q_all = queries.reshape(shape4)
    k_all = keys.reshape(shape4)
    v_all = values.reshape(shape4)
    prompt_k = text_k.reshape(NSEG, TXT, HEADS, HD)
    prompt_v = text_v.reshape(NSEG, TXT, HEADS, HD)
    bounds = jnp.cumsum(seg_frames)
    segment_of = jnp.sum((jnp.arange(FRAMES, dtype=jnp.int32)[:, None] >= bounds[None, :]).astype(jnp.int32), axis=1)
    blank = jnp.zeros((1, FT, HEADS, HD), keys.dtype)
    k_pad = jnp.concatenate([blank, k_all, blank])
    v_pad = jnp.concatenate([blank, v_all, blank])

    def front(carry, frame):
        grad_tk, grad_tv = carry
        q32 = lax.dynamic_index_in_dim(q_all, frame, 0, keepdims=False).astype(jnp.float32)
        k32 = lax.dynamic_slice_in_dim(k_pad, frame, 3, 0).reshape(3 * FT, HEADS, HD).astype(jnp.float32)
        v32 = lax.dynamic_slice_in_dim(v_pad, frame, 3, 0).reshape(3 * FT, HEADS, HD).astype(jnp.float32)
        key_frames = frame - 1 + jnp.arange(3 * FT, dtype=jnp.int32) // FT
        inside = (key_frames >= 0) & (key_frames < FRAMES)
        scores = jnp.einsum('qhd,khd->hqk', q32, k32) * scale
        scores = jnp.where(inside[None, None, :], scores, -jnp.inf)
        probs, lse = normalize(scores)
        rounded = keep_bf16(probs)
        self_out = jnp.einsum('hqk,khd->qhd', rounded, v32)
        seg = segment_of[frame]
        tk32 = lax.dynamic_index_in_dim(prompt_k, seg, 0, keepdims=False).astype(jnp.float32)
        tv32 = lax.dynamic_index_in_dim(prompt_v, seg, 0, keepdims=False).astype(jnp.float32)
        used = jnp.arange(TXT, dtype=jnp.int32) < text_len[seg]
        c_scores = jnp.einsum('qhd,khd->hqk', q32, tk32) * scale
        c_scores = jnp.where(used[None, None, :], c_scores, -jnp.inf)
        c_probs, c_lse = normalize(c_scores)
        c_rounded = keep_bf16(c_probs)
        cross_out = jnp.einsum('hqk,khd->qhd', c_rounded, tv32)
        grad = (self_out + cross_out).astype(jnp.bfloat16)
        g32 = lax.optimization_barrier(grad).astype(jnp.float32)
        self_delta = jnp.einsum('qhd,qhd->hq', g32, self_out)
        cross_delta = jnp.einsum('qhd,qhd->hq', g32, cross_out)
        dprob = jnp.einsum('qhd,khd->hqk', g32, v32)
        dscore = keep_bf16(probs * (dprob - self_delta[:, :, None]))
        c_dprob = jnp.einsum('qhd,khd->hqk', g32, tv32)
        c_dscore = keep_bf16(c_probs * (c_dprob - cross_delta[:, :, None]))
        dq_self = scale * jnp.einsum('hqk,khd->qhd', dscore, k32)
        dq_cross = scale * jnp.einsum('hqk,khd->qhd', c_dscore, tk32)
        grad_q = (dq_self + dq_cross).astype(jnp.bfloat16)
        part_tk = scale * jnp.einsum('hqk,qhd->khd', c_dscore, q32)
        part_tv = jnp.einsum('hqk,qhd->khd', c_rounded, g32)
        grad_tk = grad_tk.at[seg].add(part_tk)
        grad_tv = grad_tv.at[seg].add(part_tv)
        return (grad_tk, grad_tv), (grad_q, grad, lse[:, :, 0], self_delta)

    zeros = jnp.zeros((NSEG, TXT, HEADS, HD), jnp.float32)
    (grad_tk, grad_tv), (grad_q, grads, lses, deltas) = lax.scan(front, (zeros, zeros), jnp.arange(FRAMES, dtype=jnp.int32))
    q_pad = jnp.concatenate([blank, q_all, blank])
    g_pad = jnp.concatenate([blank, grads, blank])
    side = jnp.zeros((1, HEADS, FT), jnp.float32)
    lse_pad = jnp.concatenate([side, lses, side])
    delta_pad = jnp.concatenate([side, deltas, side])

    def back(frame):
        qw = lax.dynamic_slice_in_dim(q_pad, frame, 3, 0).reshape(3 * FT, HEADS, HD).astype(jnp.float32)
        gw = lax.dynamic_slice_in_dim(g_pad, frame, 3, 0).reshape(3 * FT, HEADS, HD).astype(jnp.float32)
        lw = lax.dynamic_slice_in_dim(lse_pad, frame, 3, 0).transpose(1, 0, 2).reshape(HEADS, 3 * FT)
        dw = lax.dynamic_slice_in_dim(delta_pad, frame, 3, 0).transpose(1, 0, 2).reshape(HEADS, 3 * FT)
        query_frames = frame - 1 + jnp.arange(3 * FT, dtype=jnp.int32) // FT
        inside = (query_frames >= 0) & (query_frames < FRAMES)
        kb = lax.dynamic_index_in_dim(k_all, frame, 0, keepdims=False).astype(jnp.float32)
        vb = lax.dynamic_index_in_dim(v_all, frame, 0, keepdims=False).astype(jnp.float32)
        scores = jnp.einsum('qhd,khd->hqk', qw, kb) * scale
        probs = jnp.where(inside[None, :, None], jnp.exp(scores - lw[:, :, None]), 0.0)
        rounded = keep_bf16(probs)
        dprob = jnp.einsum('qhd,khd->hqk', gw, vb)
        dscore = keep_bf16(probs * (dprob - dw[:, :, None]))
        grad_k = (scale * jnp.einsum('hqk,qhd->khd', dscore, qw)).astype(jnp.bfloat16)
        grad_v = jnp.einsum('hqk,qhd->khd', rounded, gw).astype(jnp.bfloat16)
        return grad_k, grad_v

    grad_k, grad_v = lax.map(back, jnp.arange(FRAMES, dtype=jnp.int32))
    return (grad_q.reshape(TOKENS, HEADS * HD), grad_k.reshape(TOKENS, HEADS * HD), grad_v.reshape(TOKENS, HEADS * HD),
            grad_tk.reshape(NSEG, TXT, HEADS * HD), grad_tv.reshape(NSEG, TXT, HEADS * HD))
```

```python
import math

import jax
import jax.numpy as jnp
from jax import lax
from jax.experimental import pallas as pl
from jax.experimental.pallas import tpu as pltpu
from jax.sharding import PartitionSpec as P

HD = 128
FT = 64
NSEG = 4
TXT = 128
NU = 8
NX = 4
NZ = 16
NF = NX * NZ
HEADS = 3
W = HEADS * HD
TOK = 128
ROWS = NU * TOK
EXT = ROWS + 2 * FT
SCALE = HD ** -0.5
EXP2 = SCALE * math.log2(math.e)
MESH = pl.DeviceIdType.MESH
VMEM_LIMIT = 56 * 1024 * 1024


def place():
    f = lax.axis_index("frame")
    u = lax.axis_index("uly")
    return f, u, lax.div(f, NZ), lax.rem(f, NZ)


def uly_peer(f, u, d):
    return (f, lax.rem(u + d, NU))


def z_peer(x, z, u, d):
    return (x * NZ + lax.rem(z + d, NZ), u)


def x_peer(f, u, d):
    return (lax.rem(f + NZ * d, NF), u)


def meet(f, u, x, z):
    barrier = pltpu.get_barrier_semaphore()
    peers = [uly_peer(f, u, d) for d in range(1, NU)]
    peers += [z_peer(x, z, u, d) for d in range(1, NZ)]
    peers += [x_peer(f, u, d) for d in range(1, NX)]
    peers += [(lax.rem(f + 1, NF), u), (lax.rem(f + NF - 1, NF), u)]
    for peer in peers:
        pl.semaphore_signal(barrier, inc=1, device_id=peer, device_id_type=MESH)
    pl.semaphore_wait(barrier, len(peers))


def remote(src, dst, send, recv, peer):
    return pltpu.make_async_remote_copy(
        src_ref=src, dst_ref=dst, send_sem=send, recv_sem=recv, device_id=peer, device_id_type=MESH
    )


def scatter_heads(q, k, v, text, hq, hk, hv, tg, a_send, a_recv, l_sem, h_send, h_recv, z_send, z_recv, x_send, x_recv):
    f, u, x, z = place()
    meet(f, u, x, z)
    local = [pltpu.make_async_copy(text, tg.at[f], l_sem.at[3])]
    zs = []
    for d in range(1, NZ):
        zs.append(remote(text, tg.at[f], z_send.at[d], z_recv.at[d], z_peer(x, z, u, d)))
    moves = []
    mine = pl.ds(pl.multiple_of(u * W, HD), W)
    for i, (src, dst, off) in enumerate(((k, hk, FT), (v, hv, FT), (q, hq, 0))):
        rows = pl.ds(pl.multiple_of(off + u * TOK, FT), TOK)
        local.append(pltpu.make_async_copy(src.at[:, mine], dst.at[rows], l_sem.at[i]))
        group = []
        for d in (4, 3, 5, 2, 6, 1, 7):
            peer = uly_peer(f, u, d)
            cols = pl.ds(pl.multiple_of(peer[1] * W, HD), W)
            group.append(remote(src.at[:, cols], dst.at[rows], a_send.at[i, d], a_recv.at[i, d], peer))
        moves.append(group)
    for c in zs + local + moves[0] + moves[1] + moves[2]:
        c.start()
    for c in zs:
        c.wait_recv()
    local[0].wait()
    xs = []
    block = pl.ds(x * NZ, NZ)
    for d in range(1, NX):
        xs.append(remote(tg.at[block], tg.at[block], x_send.at[d], x_recv.at[d], x_peer(f, u, d)))
    for c in xs:
        c.start()
    for c in moves[0] + moves[1]:
        c.wait_recv()
    local[1].wait()
    local[2].wait()
    after = (lax.rem(f + 1, NF), u)
    before = (lax.rem(f + NF - 1, NF), u)
    halo = []
    for i, ref in enumerate((hk, hv)):
        halo.append(remote(ref.at[pl.ds(FT, FT)], ref.at[pl.ds(FT + ROWS, FT)], h_send.at[i, 0], h_recv.at[i, 0], before))
        halo.append(remote(ref.at[pl.ds(ROWS, FT)], ref.at[pl.ds(0, FT)], h_send.at[i, 1], h_recv.at[i, 1], after))
    for c in halo:
        c.start()
    for c in moves[2]:
        c.wait_recv()
    local[3].wait()
    for c in halo + xs:
        c.wait_recv()
    for c in zs + moves[0] + moves[1] + moves[2] + xs + halo:
        c.wait_send()


def dot(a, b, ca, cb):
    return lax.dot_general(a, b, (((ca,), (cb,)), ((), ())), preferred_element_type=jnp.float32)


def softmax(scores):
    top = jnp.max(scores, axis=-1, keepdims=True)
    e = jnp.exp2((scores - top) * EXP2)
    return e * (1.0 / jnp.sum(e, axis=-1, keepdims=True))


def attention(lens, segs, hq, hk, hv, tg, dq, dk, dv, edge, halo, gout, t32, kv32, kv16, acc_k, acc_v, acc_t):
    f = lax.axis_index("frame")
    b0 = segs[0]
    b1 = b0 + segs[1]
    b2 = b1 + segs[2]
    b3 = b2 + segs[3]
    for h in range(HEADS):
        t32[h] = tg[:, :, h * HD : (h + 1) * HD].reshape(NF * 16, HD).astype(jnp.float32)
        for c in range(2):
            for s in range(NSEG):
                for t in range(2):
                    kv32[h, c, s, pl.ds(t, NF, stride=2), :] = t32[h, pl.ds(c * 8 + s * 2 + t, NF, stride=16), :]
    kv16[...] = kv32[...].astype(jnp.bfloat16)
    acc_k[...] = jnp.zeros_like(acc_k)
    acc_v[...] = jnp.zeros_like(acc_v)
    acc_t[...] = jnp.zeros_like(acc_t)
    row = lax.broadcasted_iota(jnp.int32, (2 * FT, 4 * FT), 0)
    col = lax.broadcasted_iota(jnp.int32, (2 * FT, 4 * FT), 1)
    tcol = lax.broadcasted_iota(jnp.int32, (FT, TXT), 1)

    def step(p, carry):
        low = jnp.logical_and(f == 0, p == 0).astype(jnp.int32)
        high = jnp.logical_and(f == NF - 1, p == ROWS // TOK - 1).astype(jnp.int32)
        bad = ((col < FT) & (row >= FT * (1 - low))) | ((col >= 3 * FT) & (row < FT * (1 + high)))
        qr = pl.ds(pl.multiple_of(p * TOK, TOK), TOK)
        kr = pl.ds(pl.multiple_of(p * TOK, TOK), 4 * FT)
        seg = []
        for a in range(2):
            frame = f * (ROWS // FT) + 2 * p + a
            s = sum((frame >= b).astype(jnp.int32) for b in (b0, b1, b2, b3))
            seg.append((s, lens[s]))
        for h in range(HEADS):
            cs = slice(h * HD, (h + 1) * HD)
            q = hq[qr, cs]
            k = hk[kr, cs]
            v = hv[kr, cs]
            probs = softmax(jnp.where(bad, -1e30, dot(q, k, 1, 1)))
            rounded = probs.astype(jnp.bfloat16)
            self_out = dot(rounded, v, 1, 0)
            parts = []
            for a in range(2):
                s, n = seg[a]
                tk = kv16[h, 0, s]
                tv = kv16[h, 1, s]
                qa = q[a * FT : (a + 1) * FT]
                cp = softmax(jnp.where(tcol < n, dot(qa, tk, 1, 1), -1e30))
                cr = cp.astype(jnp.bfloat16)
                parts.append((s, tk, tv, qa, cp, cr, dot(cr, tv, 1, 0)))
            cross_out = jnp.concatenate([parts[0][-1], parts[1][-1]], axis=0)
            g = (self_out + cross_out).astype(jnp.bfloat16)
            g32 = g.astype(jnp.float32)
            s_delta = jnp.sum(g32 * self_out, axis=-1, keepdims=True)
            c_delta = jnp.sum(g32 * cross_out, axis=-1, keepdims=True)
            ds = (probs * (dot(g, v, 1, 1) - s_delta)).astype(jnp.bfloat16)
            dq_self = dot(ds, k, 1, 0)
            acc_k[h, kr] += dot(ds, q, 0, 0)
            acc_v[h, kr] += dot(rounded, g, 0, 0)
            dq_cross = []
            for a in range(2):
                s, tk, tv, qa, cp, cr, _ = parts[a]
                half = slice(a * FT, (a + 1) * FT)
                ga = g[half]
                dsc = (cp * (dot(ga, tv, 1, 1) - c_delta[half])).astype(jnp.bfloat16)
                dq_cross.append(dot(dsc, tk, 1, 0))
                acc_t[h, 0, s] += dot(dsc, qa, 0, 0)
                acc_t[h, 1, s] += dot(cr, ga, 0, 0)
            total = dq_self + jnp.concatenate(dq_cross, axis=0)
            dq[qr, cs] = (total * SCALE).astype(jnp.bfloat16)
        return carry

    lax.fori_loop(0, ROWS // TOK, step, 0)
    for h in range(HEADS):
        cs = slice(h * HD, (h + 1) * HD)
        for i, (acc, out, scale) in enumerate(((acc_k, dk, SCALE), (acc_v, dv, 1.0))):
            out[:, cs] = (acc[h, FT : FT + ROWS] * scale).astype(jnp.bfloat16)
            edge[2 * i, :, cs] = acc[h, FT : 2 * FT] * scale
            edge[2 * i + 1, :, cs] = acc[h, ROWS : ROWS + FT] * scale
            halo[2 * i, :, cs] = (acc[h, 0:FT] * scale).astype(jnp.bfloat16)
            halo[2 * i + 1, :, cs] = (acc[h, FT + ROWS : EXT] * scale).astype(jnp.bfloat16)
        for c in range(2):
            scale = SCALE if c == 0 else 1.0
            for s in range(NSEG):
                for t in range(2):
                    t32[h, pl.ds(c * 8 + s * 2 + t, NF, stride=16), :] = acc_t[h, c, s, pl.ds(t, NF, stride=2), :] * scale
        gout[:, :, cs] = t32[h].astype(jnp.bfloat16).reshape(NF, 16, HD)


def gather_heads(
    dq, dk, dv, edge, halo, gt, oq, ok, ov, og,
    kbuf, vbuf, hrecv, rx, s1, rz,
    a_send, a_recv, l_sem, h_send, h_recv, z_send, z_recv, x_send, x_recv,
):
    f, u, x, z = place()
    meet(f, u, x, z)
    after = (lax.rem(f + 1, NF), u)
    before = (lax.rem(f + NF - 1, NF), u)
    hs = []
    for i in range(2):
        hs.append(remote(halo.at[2 * i], hrecv.at[2 * i + 1], h_send.at[2 * i], h_recv.at[2 * i], before))
        hs.append(remote(halo.at[2 * i + 1], hrecv.at[2 * i], h_send.at[2 * i + 1], h_recv.at[2 * i + 1], after))
    xs = []
    for d in range(1, NX):
        peer = x_peer(f, u, d)
        block = pl.ds(lax.rem(x + d, NX) * NZ, NZ)
        xs.append(remote(gt.at[block], rx.at[d - 1], x_send.at[d], x_recv.at[d], peer))
    stage = [
        pltpu.make_async_copy(dk, kbuf, l_sem.at[0]),
        pltpu.make_async_copy(dv, vbuf, l_sem.at[1]),
    ]
    moves, local = [], []
    mine = pl.ds(pl.multiple_of(u * W, HD), W)
    own = pl.ds(pl.multiple_of(u * TOK, TOK), TOK)
    for i, (src, dst) in enumerate(((dq, oq), (kbuf, ok), (vbuf, ov))):
        local.append(pltpu.make_async_copy(src.at[own], dst.at[:, mine], l_sem.at[2 + i]))
        group = []
        for d in (4, 3, 5, 2, 6, 1, 7):
            peer = uly_peer(f, u, d)
            rows = pl.ds(pl.multiple_of(peer[1] * TOK, TOK), TOK)
            group.append(remote(src.at[rows], dst.at[:, mine], a_send.at[i, d], a_recv.at[i, d], peer))
        moves.append(group)
    for c in hs + xs + stage + moves[0] + local[:1]:
        c.start()
    for c in hs:
        c.wait_recv()
    for c in stage:
        c.wait()
    kbuf[0:FT] = (edge[0] + hrecv[0].astype(jnp.float32)).astype(jnp.bfloat16)
    kbuf[ROWS - FT : ROWS] = (edge[1] + hrecv[1].astype(jnp.float32)).astype(jnp.bfloat16)
    vbuf[0:FT] = (edge[2] + hrecv[2].astype(jnp.float32)).astype(jnp.bfloat16)
    vbuf[ROWS - FT : ROWS] = (edge[3] + hrecv[3].astype(jnp.float32)).astype(jnp.bfloat16)
    for c in moves[1] + moves[2] + local[1:]:
        c.start()
    for c in xs:
        c.wait_recv()
    total = gt[pl.ds(x * NZ, NZ)].astype(jnp.float32)
    for d in range(1, NX):
        total = total + rx[d - 1].astype(jnp.float32)
    s1[...] = total.astype(jnp.bfloat16)
    zs = []
    for d in range(1, NZ):
        zs.append(remote(s1.at[lax.rem(z + d, NZ)], rz.at[d - 1], z_send.at[d], z_recv.at[d], z_peer(x, z, u, d)))
    for c in zs:
        c.start()
    for c in zs:
        c.wait_recv()
    last = s1[z].astype(jnp.float32)
    for d in range(1, NZ):
        last = last + rz[d - 1].astype(jnp.float32)
    og[...] = last
    for g in moves:
        for c in g:
            c.wait_recv()
    for c in local:
        c.wait()
    for c in hs + xs + zs + moves[0] + moves[1] + moves[2]:
        c.wait_send()


def body(queries, keys, values, text_k, text_v, text_len, seg_frames):
    bf16, f32 = jnp.bfloat16, jnp.float32
    hbm = pl.BlockSpec(memory_space=pl.ANY)
    vmem = pl.BlockSpec(memory_space=pltpu.VMEM)
    smem = pl.BlockSpec(memory_space=pltpu.SMEM)
    dma = pltpu.SemaphoreType.DMA
    S = jax.ShapeDtypeStruct
    text = jnp.concatenate([text_k.reshape(8, W), text_v.reshape(8, W)], axis=0)
    hq, hk, hv, tg = pl.pallas_call(
        scatter_heads,
        out_shape=(S((ROWS, W), bf16), S((EXT, W), bf16), S((EXT, W), bf16), S((NF, 16, W), bf16)),
        in_specs=[hbm, hbm, hbm, hbm],
        out_specs=(hbm, hbm, hbm, hbm),
        scratch_shapes=[
            dma((3, NU)), dma((3, NU)), dma((4,)), dma((2, 2)), dma((2, 2)),
            dma((NZ,)), dma((NZ,)), dma((NX,)), dma((NX,)),
        ],
        compiler_params=pltpu.CompilerParams(collective_id=0, has_side_effects=True, vmem_limit_bytes=VMEM_LIMIT),
        name="scatter_heads",
    )(queries, keys, values, text)
    dq, dk, dv, edge, halo, gt = pl.pallas_call(
        attention,
        out_shape=(
            S((ROWS, W), bf16), S((ROWS, W), bf16), S((ROWS, W), bf16),
            S((4, FT, W), f32), S((4, FT, W), bf16), S((NF, 16, W), bf16),
        ),
        in_specs=[smem, smem, vmem, vmem, vmem, vmem],
        out_specs=(vmem,) * 6,
        scratch_shapes=[
            pltpu.VMEM((HEADS, NF * 16, HD), f32),
            pltpu.VMEM((HEADS, 2, NSEG, TXT, HD), f32),
            pltpu.VMEM((HEADS, 2, NSEG, TXT, HD), bf16),
            pltpu.VMEM((HEADS, EXT, HD), f32),
            pltpu.VMEM((HEADS, EXT, HD), f32),
            pltpu.VMEM((HEADS, 2, NSEG, TXT, HD), f32),
        ],
        compiler_params=pltpu.CompilerParams(vmem_limit_bytes=VMEM_LIMIT),
        name="attention",
    )(text_len, seg_frames, hq, hk, hv, tg)
    oq, ok, ov, og = pl.pallas_call(
        gather_heads,
        out_shape=(S((TOK, NU * W), bf16),) * 3 + (S((16, W), f32),),
        in_specs=[hbm, hbm, hbm, vmem, vmem, vmem],
        out_specs=(hbm, hbm, hbm, vmem),
        scratch_shapes=[
            pltpu.VMEM((ROWS, W), bf16), pltpu.VMEM((ROWS, W), bf16), pltpu.VMEM((4, FT, W), bf16),
            pltpu.VMEM((NX - 1, NZ, 16, W), bf16), pltpu.VMEM((NZ, 16, W), bf16), pltpu.VMEM((NZ - 1, 16, W), bf16),
            dma((3, NU)), dma((3, NU)), dma((5,)), dma((4,)), dma((4,)),
            dma((NZ,)), dma((NZ,)), dma((NX,)), dma((NX,)),
        ],
        compiler_params=pltpu.CompilerParams(collective_id=1, has_side_effects=True, vmem_limit_bytes=VMEM_LIMIT),
        name="gather_heads",
    )(dq, dk, dv, edge, halo, gt)
    og = og.reshape(2, NSEG, 2, W)
    return oq, ok, ov, og[0], og[1]


def solution(mesh):
    rows = P(("frame", "uly"), None)
    text = P(None, "frame", "uly")
    return jax.shard_map(
        body,
        mesh=mesh,
        in_specs=(rows, rows, rows, text, text, P(), P()),
        out_specs=(rows, rows, rows, text, text),
        check_vma=False,
    )
```

```python
import math

import jax
import jax.numpy as jnp
from jax import lax
from jax.experimental import pallas as pl
from jax.experimental.pallas import tpu as pltpu
from jax.sharding import PartitionSpec as P

HD = 128
FT = 64
NSEG = 4
TXT = 128
NU = 8
NX = 4
NZ = 16
NF = NX * NZ
HEADS = 3
W = HEADS * HD
TOK = 128
ROWS = NU * TOK
EXT = ROWS + 2 * FT
TILES = EXT // TOK
SCALE = HD ** -0.5
EXP2 = SCALE * math.log2(math.e)
MESH = pl.DeviceIdType.MESH
VMEM_LIMIT = 56 * 1024 * 1024
FAR_FIRST = (4, 3, 5, 2, 6, 1, 7)
BF16 = jnp.bfloat16
F32 = jnp.float32


def place():
    f = lax.axis_index("frame")
    u = lax.axis_index("uly")
    return f, u, lax.div(f, NZ), lax.rem(f, NZ)


def uly_peer(f, u, d):
    return (f, lax.rem(u + d, NU))


def z_peer(x, z, u, d):
    return (x * NZ + lax.rem(z + d, NZ), u)


def x_peer(f, u, d):
    return (lax.rem(f + NZ * d, NF), u)


def meet(f, u, x, z):
    barrier = pltpu.get_barrier_semaphore()
    peers = [uly_peer(f, u, d) for d in range(1, NU)]
    peers += [z_peer(x, z, u, d) for d in range(1, NZ)]
    peers += [x_peer(f, u, d) for d in range(1, NX)]
    peers += [(lax.rem(f + 1, NF), u), (lax.rem(f + NF - 1, NF), u)]
    for peer in peers:
        pl.semaphore_signal(barrier, inc=1, device_id=peer, device_id_type=MESH)
    pl.semaphore_wait(barrier, len(peers))


def remote(src, dst, send, recv, peer):
    return pltpu.make_async_remote_copy(
        src_ref=src, dst_ref=dst, send_sem=send, recv_sem=recv, device_id=peer, device_id_type=MESH
    )


def dot(a, b, ca, cb):
    return lax.dot_general(a, b, (((ca,), (cb,)), ((), ())), preferred_element_type=F32)


def softmax(scores):
    top = jnp.max(scores, axis=0, keepdims=True)
    e = jnp.exp2((scores - top) * EXP2)
    return e * (1.0 / jnp.sum(e, axis=0, keepdims=True))


def bounds_of(segs):
    b0 = segs[0]
    b1 = b0 + segs[1]
    b2 = b1 + segs[2]
    return b0, b1, b2


def segment(frame, bounds):
    return sum((frame >= b).astype(jnp.int32) for b in bounds)


def text_in(tg, t32, kv32, tkv, tkvT):
    for h in range(HEADS):
        t32[...] = tg[h].reshape(NF * 16, HD).astype(F32)
        for c in range(2):
            for s in range(NSEG):
                for t in range(2):
                    kv32[c, s, pl.ds(t, NF, stride=2), :] = t32[pl.ds(c * 8 + s * 2 + t, NF, stride=16), :]
                part = kv32[c, s]
                tkv[h, c, s] = part.astype(BF16)
                tkvT[h, c, s] = part.T.astype(BF16)


def turn(src, dst, tiles):
    for t in tiles:
        dst[:, t * TOK : (t + 1) * TOK] = src[t * TOK : (t + 1) * TOK, :].T


def pairs_step(pairs, f, lens, bounds, hq, hk, hv, kT, vT, tkv, tkvT, dq, acc_k, acc_v, sc, pc, gT):
    row = lax.broadcasted_iota(jnp.int32, (4 * FT, 2 * FT), 0)
    lane = lax.broadcasted_iota(jnp.int32, (4 * FT, 2 * FT), 1)
    trow = lax.broadcasted_iota(jnp.int32, (TXT, 2 * FT), 0)
    left = lax.broadcasted_iota(jnp.int32, (TXT, 2 * FT), 1) < FT
    work = []
    for p in pairs:
        low = jnp.logical_and(f == 0, p == 0).astype(jnp.int32)
        high = jnp.logical_and(f == NF - 1, p == ROWS // TOK - 1).astype(jnp.int32)
        bad = ((row < FT) & (lane >= FT * (1 - low))) | ((row >= 3 * FT) & (lane < FT * (1 + high)))
        qr = pl.ds(pl.multiple_of(p * TOK, TOK), TOK)
        kr = pl.ds(pl.multiple_of(p * TOK, TOK), 4 * FT)
        s0 = segment(f * (ROWS // FT) + 2 * p, bounds)
        s1 = segment(f * (ROWS // FT) + 2 * p + 1, bounds)
        n = jnp.where(left, lens[s0], lens[s1])
        work.append((bad, qr, kr, s0, s1, n))
    qs = [hq[w[1], :] for w in work]
    ks = [hk[w[2], :] for w in work]
    vs = [hv[w[2], :] for w in work]
    ss = [dot(k, q, 1, 1) for k, q in zip(ks, qs)]
    cs = [
        jnp.where(left, dot(tkv[0, w[3]], q, 1, 1), dot(tkv[0, w[4]], q, 1, 1)) for w, q in zip(work, qs)
    ]
    ps = [softmax(jnp.where(w[0], -1e30, s)) for w, s in zip(work, ss)]
    cps = [softmax(jnp.where(trow < w[5], c, -1e30)) for w, c in zip(work, cs)]
    p16 = [p.astype(BF16) for p in ps]
    cp16 = [c.astype(BF16) for c in cps]
    so = [dot(vT[:, w[2]], p, 1, 0) for w, p in zip(work, p16)]
    co = [
        jnp.where(left, dot(tkvT[1, w[3]], c, 1, 0), dot(tkvT[1, w[4]], c, 1, 0)) for w, c in zip(work, cp16)
    ]
    g16 = [(a + b).astype(BF16) for a, b in zip(so, co)]
    sd = [jnp.sum(g.astype(F32) * a, axis=0, keepdims=True) for g, a in zip(g16, so)]
    cd = [jnp.sum(g.astype(F32) * a, axis=0, keepdims=True) for g, a in zip(g16, co)]
    ds = [(p * (dot(v, g, 1, 0) - d)).astype(BF16) for p, v, g, d in zip(ps, vs, g16, sd)]
    dcs = [
        (c * (jnp.where(left, dot(tkv[1, w[3]], g, 1, 0), dot(tkv[1, w[4]], g, 1, 0)) - d)).astype(BF16)
        for c, w, g, d in zip(cps, work, g16, cd)
    ]
    dqs = [
        dot(kT[:, w[2]], s, 1, 0) + jnp.where(left, dot(tkvT[0, w[3]], c, 1, 0), dot(tkvT[0, w[4]], c, 1, 0))
        for w, s, c in zip(work, ds, dcs)
    ]
    dks = [acc_k[w[2], :] + dot(s, q, 1, 0) for w, s, q in zip(work, ds, qs)]
    dvs = [acc_v[w[2], :] + dot(p, g, 1, 1) for w, p, g in zip(work, p16, g16)]
    for i, w in enumerate(work):
        dq[w[1], :] = (dqs[i] * SCALE).T.astype(BF16)
        acc_k[w[2], :] = dks[i]
        acc_v[w[2], :] = dvs[i]
        sc[:, w[1]] = dcs[i]
        pc[:, w[1]] = cp16[i]
        gT[:, w[1]] = g16[i]


def text_out(f, bounds, hq, sc, pc, gT, t32, kv32, gt):
    frame = f * (ROWS // FT) + lax.broadcasted_iota(jnp.int32, (16, ROWS), 1) // FT
    seg = segment(frame, bounds)
    q = hq[...]
    g = gT[...]
    for s in range(NSEG):
        on = jnp.broadcast_to((seg == s).astype(F32).astype(BF16)[0:1], (TXT, ROWS))
        kv32[0, s] = dot(sc[...] * on, q, 1, 0) * SCALE
        kv32[1, s] = dot(pc[...] * on, g, 1, 1)
    for c in range(2):
        for s in range(NSEG):
            for t in range(2):
                t32[pl.ds(c * 8 + s * 2 + t, NF, stride=16), :] = kv32[c, s, pl.ds(t, NF, stride=2), :]
    gt[...] = t32[...].astype(BF16).reshape(NF, 16, HD)


def fused(
    lens, segs, q, k, v, tk_in, tv_in, oq, ok, ov, ogk, ogv,
    slab32, slab, hq, hk, hv, tg, t32, kv32, tkv, tkvT, kT, vT, acc_k, acc_v, sc, pc, gT,
    dq, dk, dv, hsend, hrecv, gt, rx, s1, rz,
    a_send, a_recv, l_sem, h_send, h_recv, z_send, z_recv, x_send, x_recv,
    b_send, b_recv, m_sem, e_send, e_recv, w_send, w_recv, y_send, y_recv,
):
    f, u, x, z = place()
    bounds = bounds_of(segs)
    after = (lax.rem(f + 1, NF), u)
    before = (lax.rem(f + NF - 1, NF), u)
    for s in range(NSEG):
        slab32[2 * s : 2 * s + 2, :] = tk_in[s].astype(F32)
        slab32[8 + 2 * s : 8 + 2 * s + 2, :] = tv_in[s].astype(F32)
    for h in range(HEADS):
        slab[h] = slab32[:, h * HD : (h + 1) * HD].astype(BF16)
    meet(f, u, x, z)

    own_text = pltpu.make_async_copy(slab, tg.at[:, f], l_sem.at[0, 3])
    zs = [remote(slab, tg.at[:, f], z_send.at[d], z_recv.at[d], z_peer(x, z, u, d)) for d in range(1, NZ)]
    block = pl.ds(x * NZ, NZ)
    xs = [
        remote(tg.at[:, block], tg.at[:, block], x_send.at[d], x_recv.at[d], x_peer(f, u, d)) for d in range(1, NX)
    ]

    def arrivals(h):
        local, moves = [], []
        for i, (src, dst, off) in enumerate(((k, hk, FT), (v, hv, FT), (q, hq, 0))):
            rows = pl.ds(pl.multiple_of(off + u * TOK, FT), TOK)
            mine = pl.ds(pl.multiple_of(u * W + h * HD, HD), HD)
            local.append(pltpu.make_async_copy(src.at[:, mine], dst.at[h, rows], l_sem.at[h, i]))
            for d in FAR_FIRST:
                peer = uly_peer(f, u, d)
                cols = pl.ds(pl.multiple_of(peer[1] * W + h * HD, HD), HD)
                moves.append(remote(src.at[:, cols], dst.at[h, rows], a_send.at[h, i, d], a_recv.at[h, i, d], peer))
        return local, moves

    def halo_in(h):
        out = []
        for i, ref in enumerate((hk, hv)):
            lo, hi = ref.at[h, pl.ds(FT, FT)], ref.at[h, pl.ds(ROWS, FT)]
            out.append(remote(lo, ref.at[h, pl.ds(FT + ROWS, FT)], h_send.at[h, i, 0], h_recv.at[h, i, 0], before))
            out.append(remote(hi, ref.at[h, pl.ds(0, FT)], h_send.at[h, i, 1], h_recv.at[h, i, 1], after))
        return out

    def halo_out(h):
        out = []
        for i in range(2):
            out.append(remote(hsend.at[h, 2 * i], hrecv.at[h, 2 * i + 1], e_send.at[h, 2 * i], e_recv.at[h, 2 * i], before))
            out.append(
                remote(hsend.at[h, 2 * i + 1], hrecv.at[h, 2 * i], e_send.at[h, 2 * i + 1], e_recv.at[h, 2 * i + 1], after)
            )
        return out

    def returns(h, i):
        src, dst = ((dq, oq), (dk, ok), (dv, ov))[i]
        cols = pl.ds(pl.multiple_of(u * W + h * HD, HD), HD)
        own = pl.ds(pl.multiple_of(u * TOK, TOK), TOK)
        local = pltpu.make_async_copy(src.at[h, own], dst.at[:, cols], m_sem.at[h, i])
        moves = []
        for d in FAR_FIRST:
            peer = uly_peer(f, u, d)
            rows = pl.ds(pl.multiple_of(peer[1] * TOK, TOK), TOK)
            moves.append(remote(src.at[h, rows], dst.at[:, cols], b_send.at[h, i, d], b_recv.at[h, i, d], peer))
        return local, moves

    def text_x(h):
        out = []
        for d in range(1, NX):
            part = pl.ds(lax.rem(x + d, NX) * NZ, NZ)
            out.append(remote(gt.at[h, part], rx.at[h, d - 1], y_send.at[h, d], y_recv.at[h, d], x_peer(f, u, d)))
        return out

    def text_z(h):
        return [
            remote(s1.at[h, lax.rem(z + d, NZ)], rz.at[h, d - 1], w_send.at[h, d], w_recv.at[h, d], z_peer(x, z, u, d))
            for d in range(1, NZ)
        ]

    def finish_edges(h):
        for c in halo_out(h):
            c.wait_recv()
        for i, (acc, out) in enumerate(((acc_k, dk), (acc_v, dv))):
            scale = SCALE if i == 0 else 1.0
            out[h, 0:FT] = (acc[h, FT : 2 * FT] * scale + hrecv[h, 2 * i].astype(F32)).astype(BF16)
            out[h, ROWS - FT : ROWS] = (acc[h, ROWS : ROWS + FT] * scale + hrecv[h, 2 * i + 1].astype(F32)).astype(BF16)
        for i in (1, 2):
            local, moves = returns(h, i)
            local.start()
            for c in moves:
                c.start()

    def text_mid(h):
        for c in text_x(h):
            c.wait_recv()
        total = gt[h, block].astype(F32)
        for d in range(1, NX):
            total = total + rx[h, d - 1].astype(F32)
        s1[h] = total.astype(BF16)
        for c in text_z(h):
            c.start()

    for c in zs:
        c.start()
    own_text.start()
    for h in range(HEADS):
        local, moves = arrivals(h)
        for c in local + moves:
            c.start()
    acc_k[...] = jnp.zeros_like(acc_k)
    acc_v[...] = jnp.zeros_like(acc_v)
    own_text.wait()
    for c in zs:
        c.wait_recv()
    for c in xs:
        c.start()

    for h in range(HEADS):
        local, moves = arrivals(h)
        for c in local:
            c.wait()
        for c in moves:
            c.wait_recv()
        halo = halo_in(h)
        for c in halo:
            c.start()
        turn(hk.at[h], kT, range(1, TILES - 1))
        turn(hv.at[h], vT, range(1, TILES - 1))
        if h == 0:
            for c in xs:
                c.wait_recv()
            text_in(tg, t32, kv32, tkv, tkvT)
        refs = (
            f, lens, bounds, hq.at[h], hk.at[h], hv.at[h], kT, vT, tkv.at[h], tkvT.at[h], dq.at[h],
            acc_k.at[h], acc_v.at[h], sc, pc, gT,
        )

        def inner(i, carry):
            pairs_step((i + 1, i + 4), *refs)
            return carry

        lax.fori_loop(0, 3, inner, 0)
        for c in halo:
            c.wait_recv()
        turn(hk.at[h], kT, (0, TILES - 1))
        turn(hv.at[h], vT, (0, TILES - 1))
        pairs_step((0, 7), *refs)
        for i, acc in enumerate((acc_k, acc_v)):
            scale = SCALE if i == 0 else 1.0
            hsend[h, 2 * i] = (acc[h, 0:FT] * scale).astype(BF16)
            hsend[h, 2 * i + 1] = (acc[h, FT + ROWS : EXT] * scale).astype(BF16)
        for c in halo_out(h):
            c.start()
        local, moves = returns(h, 0)
        local.start()
        for c in moves:
            c.start()
        text_out(f, bounds, hq.at[h], sc, pc, gT, t32, kv32, gt.at[h])
        for c in text_x(h):
            c.start()
        dk[h, FT : ROWS - FT] = (acc_k[h, 2 * FT : ROWS] * SCALE).astype(BF16)
        dv[h, FT : ROWS - FT] = acc_v[h, 2 * FT : ROWS].astype(BF16)
        finish_edges(h)
        if h > 0:
            text_mid(h - 1)
    text_mid(HEADS - 1)
    for h in range(HEADS):
        for c in text_z(h):
            c.wait_recv()
        last = s1[h, z].astype(F32)
        for d in range(1, NZ):
            last = last + rz[h, d - 1].astype(F32)
        cols = slice(h * HD, (h + 1) * HD)
        for s in range(NSEG):
            ogk[s, :, cols] = last[2 * s : 2 * s + 2]
            ogv[s, :, cols] = last[8 + 2 * s : 8 + 2 * s + 2]
    for c in zs + xs:
        c.wait_send()
    for h in range(HEADS):
        for c in arrivals(h)[1] + halo_in(h) + halo_out(h) + text_x(h) + text_z(h):
            c.wait_send()
        for i in range(3):
            local, moves = returns(h, i)
            local.wait()
            for c in moves:
                c.wait()


def body(queries, keys, values, text_k, text_v, text_len, seg_frames):
    hbm = pl.BlockSpec(memory_space=pl.ANY)
    vmem = pl.BlockSpec(memory_space=pltpu.VMEM)
    smem = pl.BlockSpec(memory_space=pltpu.SMEM)
    dma = pltpu.SemaphoreType.DMA
    S = jax.ShapeDtypeStruct
    V = pltpu.VMEM
    H = HEADS
    return pl.pallas_call(
        fused,
        out_shape=(S((TOK, NU * W), BF16),) * 3 + (S((NSEG, 2, W), F32),) * 2,
        in_specs=[smem, smem, hbm, hbm, hbm, vmem, vmem],
        out_specs=(hbm, hbm, hbm, vmem, vmem),
        scratch_shapes=[
            V((16, W), F32), V((H, 16, HD), BF16),
            V((H, ROWS, HD), BF16), V((H, EXT, HD), BF16), V((H, EXT, HD), BF16),
            V((H, NF, 16, HD), BF16), V((NF * 16, HD), F32), V((2, NSEG, TXT, HD), F32),
            V((H, 2, NSEG, TXT, HD), BF16), V((H, 2, NSEG, HD, TXT), BF16),
            V((HD, EXT), BF16), V((HD, EXT), BF16),
            V((H, EXT, HD), F32), V((H, EXT, HD), F32),
            V((TXT, ROWS), BF16), V((TXT, ROWS), BF16), V((HD, ROWS), BF16),
            V((H, ROWS, HD), BF16), V((H, ROWS, HD), BF16), V((H, ROWS, HD), BF16),
            V((H, 4, FT, HD), BF16), V((H, 4, FT, HD), BF16),
            V((H, NF, 16, HD), BF16), V((H, NX - 1, NZ, 16, HD), BF16), V((H, NZ, 16, HD), BF16),
            V((H, NZ - 1, 16, HD), BF16),
            dma((H, 3, NU)), dma((H, 3, NU)), dma((H, 4)), dma((H, 2, 2)), dma((H, 2, 2)),
            dma((NZ,)), dma((NZ,)), dma((NX,)), dma((NX,)),
            dma((H, 3, NU)), dma((H, 3, NU)), dma((H, 3)), dma((H, 4)), dma((H, 4)),
            dma((H, NZ)), dma((H, NZ)), dma((H, NX)), dma((H, NX)),
        ],
        compiler_params=pltpu.CompilerParams(collective_id=0, has_side_effects=True, vmem_limit_bytes=VMEM_LIMIT),
        name="windowed_attention",
    )(text_len, seg_frames, queries, keys, values, text_k, text_v)


def solution(mesh):
    rows = P(("frame", "uly"), None)
    text = P(None, "frame", "uly")
    return jax.shard_map(
        body,
        mesh=mesh,
        in_specs=(rows, rows, rows, text, text, P(), P()),
        out_specs=(rows, rows, rows, text, text),
        check_vma=False,
    )
```

```python
import math

import jax
import jax.numpy as jnp
from jax import lax
from jax.experimental import pallas as pl
from jax.experimental.pallas import tpu as pltpu
from jax.sharding import PartitionSpec as P

HD = 128
FT = 64
NSEG = 4
TXT = 128
NU = 8
NX = 4
NZ = 16
NF = NX * NZ
HEADS = 3
W = HEADS * HD
TOK = 128
ROWS = NU * TOK
EXT = ROWS + 2 * FT
TILES = EXT // TOK
SCALE = HD ** -0.5
EXP2 = SCALE * math.log2(math.e)
QUAD = 4
FAR = (4, 12, 8)
NEAR = (1, 15, 2)
MESH = pl.DeviceIdType.MESH
VMEM_LIMIT = 56 * 1024 * 1024
FAR_FIRST = (4, 3, 5, 2, 6, 1, 7)
GROUPS = (pl.ds(0, 1), pl.ds(1, 2))
CHUNKS = 4
BF16 = jnp.bfloat16
F32 = jnp.float32


def place():
    f = lax.axis_index("frame")
    u = lax.axis_index("uly")
    return f, u, lax.div(f, NZ), lax.rem(f, NZ)


def slot(z):
    return lax.rem(z, QUAD) * QUAD + lax.div(z, QUAD)


def uly_peer(f, u, d):
    return (f, lax.rem(u + d, NU))


def z_peer(x, z, u, d):
    return (x * NZ + lax.rem(z + d, NZ), u)


def x_peer(f, u, d):
    return (lax.rem(f + NZ * d, NF), u)


def greet(sem, peer):
    pl.semaphore_signal(sem, inc=1, device_id=peer, device_id_type=MESH)


def each(first, last, act):
    def one(i, carry):
        act(i)
        return carry

    lax.fori_loop(first, last, one, 0)


def meet(f, u, x, z, ready):
    barrier = pltpu.get_barrier_semaphore()
    for d in range(1, NU):
        greet(barrier, uly_peer(f, u, d))
    each(z + 1, NZ, lambda i: greet(barrier, (x * NZ + i, u)))
    each(x + 1, NX, lambda i: greet(barrier, (i * NZ + z, u)))

    @pl.when(z == 0)
    def _():
        greet(barrier, (lax.rem(f + NF - 1, NF), u))

    pl.semaphore_wait(barrier, NU - 1 + z + x + (z == NZ - 1).astype(jnp.int32))
    each(0, z, lambda i: greet(ready, (x * NZ + i, u)))
    each(0, x, lambda i: greet(ready, (i * NZ + z, u)))

    @pl.when(z == NZ - 1)
    def _():
        greet(ready, (lax.rem(f + 1, NF), u))


def remote(src, dst, send, recv, peer):
    return pltpu.make_async_remote_copy(
        src_ref=src, dst_ref=dst, send_sem=send, recv_sem=recv, device_id=peer, device_id_type=MESH
    )


def dot(a, b, ca, cb):
    return lax.dot_general(a, b, (((ca,), (cb,)), ((), ())), preferred_element_type=F32)


def softmax(scores):
    top = jnp.max(scores, axis=0, keepdims=True)
    e = jnp.exp2((scores - top) * EXP2)
    return e * (1.0 / jnp.sum(e, axis=0, keepdims=True))


def bounds_of(segs):
    b0 = segs[0]
    b1 = b0 + segs[1]
    b2 = b1 + segs[2]
    return b0, b1, b2


def segment(frame, bounds):
    return sum((frame >= b).astype(jnp.int32) for b in bounds)


def text_in(tg, t32, kv32, tkv, tkvT):
    t32[...] = tg[...].reshape(NF * 16, HD).astype(F32)
    for c in range(2):
        for s in range(NSEG):
            for t in range(2):
                kv32[c, s, pl.ds(t, NF, stride=2), :] = t32[pl.ds(c * 8 + s * 2 + t, NF, stride=16), :]
            part = kv32[c, s]
            tkv[c, s] = part.astype(BF16)
            tkvT[c, s] = part.T.astype(BF16)


def turn(src, dst, tiles):
    for t in tiles:
        dst[:, t * TOK : (t + 1) * TOK] = src[t * TOK : (t + 1) * TOK, :].T


def halves(left, c):
    none = jnp.zeros_like(c)
    return jnp.concatenate([jnp.where(left, c, none), jnp.where(left, none, c)], axis=0)


def pairs_step(pairs, f, lens, bounds, hq, hk, hv, kT, vT, tkv, tkvT, dq, acc_k, acc_v, sc, pc, gT):
    row = lax.broadcasted_iota(jnp.int32, (4 * FT, 2 * FT), 0)
    lane = lax.broadcasted_iota(jnp.int32, (4 * FT, 2 * FT), 1)
    place_of = lax.broadcasted_iota(jnp.int32, (TXT, 2 * FT), 0)
    trow = (place_of & 97) | ((place_of & 6) << 2) | ((place_of & 24) >> 2)
    left = lax.broadcasted_iota(jnp.int32, (TXT, 2 * FT), 1) < FT
    work = []
    for p in pairs:
        low = jnp.logical_and(f == 0, p == 0).astype(jnp.int32)
        high = jnp.logical_and(f == NF - 1, p == ROWS // TOK - 1).astype(jnp.int32)
        bad = ((row < FT) & (lane >= FT * (1 - low))) | ((row >= 3 * FT) & (lane < FT * (1 + high)))
        qr = pl.ds(pl.multiple_of(p * TOK, TOK), TOK)
        kr = pl.ds(pl.multiple_of(p * TOK, TOK), 4 * FT)
        s0 = segment(f * (ROWS // FT) + 2 * p, bounds)
        s1 = segment(f * (ROWS // FT) + 2 * p + 1, bounds)
        n = jnp.where(left, lens[s0], lens[s1])
        work.append((bad, qr, kr, s0, s1, n))
    qs = [hq[w[1], :] for w in work]
    ks = [hk[w[2], :] for w in work]
    vs = [hv[w[2], :] for w in work]
    ss = [dot(k, q, 1, 1) for k, q in zip(ks, qs)]
    cs = [
        jnp.where(left, dot(tkv[0, w[3]], q, 1, 1), dot(tkv[0, w[4]], q, 1, 1)) for w, q in zip(work, qs)
    ]
    ps = [softmax(jnp.where(w[0], -1e30, s)) for w, s in zip(work, ss)]
    cps = [softmax(jnp.where(trow < w[5], c, -1e30)) for w, c in zip(work, cs)]
    p16 = [p.astype(BF16) for p in ps]
    cp16 = [c.astype(BF16) for c in cps]
    so = [dot(vT[:, w[2]], p, 1, 0) for w, p in zip(work, p16)]
    co = [
        dot(jnp.concatenate([tkvT[1, w[3]], tkvT[1, w[4]]], axis=1), halves(left, c), 1, 0) for w, c in zip(work, cp16)
    ]
    g16 = [(a + b).astype(BF16) for a, b in zip(so, co)]
    sd = [jnp.sum(g.astype(F32) * a, axis=0, keepdims=True) for g, a in zip(g16, so)]
    cd = [jnp.sum(g.astype(F32) * a, axis=0, keepdims=True) for g, a in zip(g16, co)]
    ds = [(p * (dot(v, g, 1, 0) - d)).astype(BF16) for p, v, g, d in zip(ps, vs, g16, sd)]
    dcs = [
        (c * (jnp.where(left, dot(tkv[1, w[3]], g, 1, 0), dot(tkv[1, w[4]], g, 1, 0)) - d)).astype(BF16)
        for c, w, g, d in zip(cps, work, g16, cd)
    ]
    dqs = [
        dot(
            jnp.concatenate([kT[:, w[2]], tkvT[0, w[3]], tkvT[0, w[4]]], axis=1),
            jnp.concatenate([s, halves(left, c)], axis=0), 1, 0,
        )
        for w, s, c in zip(work, ds, dcs)
    ]
    dks = [acc_k[w[2], :] + dot(s, q, 1, 0) for w, s, q in zip(work, ds, qs)]
    dvs = [acc_v[w[2], :] + dot(p, g, 1, 1) for w, p, g in zip(work, p16, g16)]
    for i, w in enumerate(work):
        dq[w[1], :] = (dqs[i] * SCALE).T.astype(BF16)
        acc_k[w[2], :] = dks[i]
        acc_v[w[2], :] = dvs[i]
        sc[:, w[1]] = dcs[i]
        pc[:, w[1]] = cp16[i]
        gT[:, w[1]] = g16[i]


def text_out(f, bounds, hq, sc, pc, gT, t32, kv32, gt):
    frame = f * (ROWS // FT) + lax.broadcasted_iota(jnp.int32, (16, ROWS), 1) // FT
    seg = segment(frame, bounds)
    q = hq[...]
    g = gT[...]
    on = [jnp.broadcast_to((seg == s).astype(F32).astype(BF16)[0:1], (TXT, ROWS)) for s in range(NSEG)]
    gk = dot(jnp.concatenate([sc[...] * m for m in on], axis=0), q, 1, 0) * SCALE
    gv = dot(jnp.concatenate([pc[...] * m for m in on], axis=0), g, 1, 1)
    for s in range(NSEG):
        kv32[0, s] = gk[s * TXT : (s + 1) * TXT]
        kv32[1, s] = gv[s * TXT : (s + 1) * TXT]
    for c in range(2):
        for s in range(NSEG):
            for t in range(2):
                t32[pl.ds(c * 8 + s * 2 + t, NF, stride=16), :] = kv32[c, s, pl.ds(t, NF, stride=2), :]
    gt[...] = t32[...].astype(BF16).reshape(NF, 16, HD)


def fused(
    lens, segs, q, k, v, tk_in, tv_in, oq, ok, ov, ogk, ogv,
    slab32, slab, hq, hk, hv, tg, t32, kv32, tkv, tkvT, kT, vT, acc_k, acc_v, sc, pc, gT,
    dq, dk, dv, hsend, hrecv, gt, rx, s1, rz,
    a_send, a_recv, l_sem, h_send, h_recv, z_send, z_recv, x_send, x_recv,
    b_send, b_recv, m_sem, e_send, e_recv, w_send, w_recv, y_send, y_recv, ready,
):
    f, u, x, z = place()
    bounds = bounds_of(segs)
    after = (lax.rem(f + 1, NF), u)
    before = (lax.rem(f + NF - 1, NF), u)
    for s in range(NSEG):
        slab32[2 * s : 2 * s + 2, :] = tk_in[s].astype(F32)
        slab32[8 + 2 * s : 8 + 2 * s + 2, :] = tv_in[s].astype(F32)
    for h in range(HEADS):
        slab[h] = slab32[:, h * HD : (h + 1) * HD].astype(BF16)
    meet(f, u, x, z, ready)

    block = pl.ds(x * NZ, NZ)

    here = x * NZ + slot(z)
    row = pl.ds(x * NZ + lax.rem(z, QUAD) * QUAD, QUAD)

    def text_own(g):
        return pltpu.make_async_copy(slab.at[GROUPS[g]], tg.at[GROUPS[g], here], l_sem.at[g, 3])

    def text_far(g):
        return [
            remote(slab.at[GROUPS[g]], tg.at[GROUPS[g], here], z_send.at[g, i], z_recv.at[g, i], z_peer(x, z, u, d))
            for i, d in enumerate(FAR)
        ]

    def text_near(g):
        part = tg.at[GROUPS[g], row]
        return [
            remote(part, part, z_send.at[g, 3 + i], z_recv.at[g, 3 + i], z_peer(x, z, u, d)) for i, d in enumerate(NEAR)
        ]

    def text_over(g):
        part = tg.at[GROUPS[g], block]
        return [remote(part, part, x_send.at[g, d], x_recv.at[g, d], x_peer(f, u, d)) for d in range(1, NX)]

    def text_first(g, lower):
        for c, d in zip(text_far(g), FAR):
            pl.when((lax.rem(z + d, NZ) < z) == lower)(c.start)

    def text_second(g):
        text_own(g).wait()
        for c in text_far(g):
            c.wait_recv()
        for c in text_near(g):
            c.start()

    def text_third(g):
        for c in text_near(g):
            c.wait_recv()
        for c in text_over(g):
            c.start()

    def arrivals(h, i):
        src, dst, off = ((k, hk, FT), (v, hv, FT), (q, hq, 0))[i]
        rows = pl.ds(pl.multiple_of(off + u * TOK, FT), TOK)
        mine = pl.ds(pl.multiple_of(u * W + h * HD, HD), HD)
        local = pltpu.make_async_copy(src.at[:, mine], dst.at[h, rows], l_sem.at[h, i])
        moves = []
        for d in FAR_FIRST:
            peer = uly_peer(f, u, d)
            cols = pl.ds(pl.multiple_of(peer[1] * W + h * HD, HD), HD)
            moves.append(remote(src.at[:, cols], dst.at[h, rows], a_send.at[h, i, d], a_recv.at[h, i, d], peer))
        return local, moves

    def issue(h, i):
        local, moves = arrivals(h, i)
        local.start()
        for c in moves:
            c.start()

    def landed(h, i):
        local, moves = arrivals(h, i)
        local.wait()
        for c in moves:
            c.wait_recv()

    def halo_in(h):
        out = []
        for i, ref in enumerate((hk, hv)):
            lo, hi = ref.at[h, pl.ds(FT, FT)], ref.at[h, pl.ds(ROWS, FT)]
            out.append(remote(lo, ref.at[h, pl.ds(FT + ROWS, FT)], h_send.at[h, i, 0], h_recv.at[h, i, 0], before))
            out.append(remote(hi, ref.at[h, pl.ds(0, FT)], h_send.at[h, i, 1], h_recv.at[h, i, 1], after))
        return out

    def halo_out(h):
        out = []
        for i in range(2):
            out.append(remote(hsend.at[h, 2 * i], hrecv.at[h, 2 * i + 1], e_send.at[h, 2 * i], e_recv.at[h, 2 * i], before))
            out.append(
                remote(hsend.at[h, 2 * i + 1], hrecv.at[h, 2 * i], e_send.at[h, 2 * i + 1], e_recv.at[h, 2 * i + 1], after)
            )
        return out

    def returns(h, i):
        src, dst = ((dq, oq), (dk, ok), (dv, ov))[i]
        cols = pl.ds(pl.multiple_of(u * W + h * HD, HD), HD)
        own = pl.ds(pl.multiple_of(u * TOK, TOK), TOK)
        local = pltpu.make_async_copy(src.at[h, own], dst.at[:, cols], m_sem.at[h, i])
        moves = []
        for d in FAR_FIRST:
            peer = uly_peer(f, u, d)
            rows = pl.ds(pl.multiple_of(peer[1] * TOK, TOK), TOK)
            moves.append(remote(src.at[h, rows], dst.at[:, cols], b_send.at[h, i, d], b_recv.at[h, i, d], peer))
        return local, moves

    def text_x(h):
        out = []
        for d in range(1, NX):
            part = pl.ds(lax.rem(x + d, NX) * NZ, NZ)
            out.append(remote(gt.at[h, part], rx.at[h, d - 1], y_send.at[h, d], y_recv.at[h, d], x_peer(f, u, d)))
        return out

    def text_z(h):
        return [
            remote(s1.at[h, slot(lax.rem(z + d, NZ))], rz.at[h, d - 1], w_send.at[h, d], w_recv.at[h, d], z_peer(x, z, u, d))
            for d in range(1, NZ)
        ]

    def give(h, i):
        local, moves = returns(h, i)
        local.start()
        for c in moves:
            c.start()

    def add_edges(h):
        for c in halo_out(h):
            c.wait_recv()
        for i, (acc, out) in enumerate(((acc_k, dk), (acc_v, dv))):
            scale = SCALE if i == 0 else 1.0
            out[h, 0:FT] = (acc[h, FT : 2 * FT] * scale + hrecv[h, 2 * i].astype(F32)).astype(BF16)
            out[h, ROWS - FT : ROWS] = (acc[h, ROWS : ROWS + FT] * scale + hrecv[h, 2 * i + 1].astype(F32)).astype(BF16)

    def text_mid(h):
        for c in text_x(h):
            c.wait_recv()
        total = gt[h, block].astype(F32)
        for d in range(1, NX):
            total = total + rx[h, d - 1].astype(F32)
        s1[h] = total.astype(BF16)
        for c in text_z(h):
            c.start()

    for g in range(2):
        text_own(g).start()
        text_first(g, True)
    for h in range(HEADS):
        for i in range(3):
            issue(h, i)
    later = NZ - 1 - z + NX - 1 - x + (z == 0).astype(jnp.int32)

    @pl.when(later > 0)
    def _():
        pl.semaphore_wait(ready, later)

    for g in range(2):
        text_first(g, False)
    acc_k[...] = jnp.zeros_like(acc_k)
    acc_v[...] = jnp.zeros_like(acc_v)

    def halo_start(h):
        landed(h, 0)
        landed(h, 1)
        for c in halo_in(h):
            c.start()

    def compute(h):
        turn(hk.at[h], kT, range(1, TILES - 1))
        turn(hv.at[h], vT, range(1, TILES - 1))
        if h < 2:
            for c in text_over(h):
                c.wait_recv()
        text_in(tg.at[h], t32, kv32, tkv.at[h], tkvT.at[h])
        landed(h, 2)
        refs = (
            f, lens, bounds, hq.at[h], hk.at[h], hv.at[h], kT, vT, tkv.at[h], tkvT.at[h], dq.at[h],
            acc_k.at[h], acc_v.at[h], sc, pc, gT,
        )

        def inner(i, carry):
            pairs_step((i + 1, i + 4), *refs)
            return carry

        lax.fori_loop(0, 3, inner, 0)
        for c in halo_in(h):
            c.wait_recv()
        turn(hk.at[h], kT, (0, TILES - 1))
        turn(hv.at[h], vT, (0, TILES - 1))
        pairs_step((0, 7), *refs)

    def halo_back(h):
        for i, acc in enumerate((acc_k, acc_v)):
            scale = SCALE if i == 0 else 1.0
            hsend[h, 2 * i] = (acc[h, 0:FT] * scale).astype(BF16)
            hsend[h, 2 * i + 1] = (acc[h, FT + ROWS : EXT] * scale).astype(BF16)
        for c in halo_out(h):
            c.start()

    def text_sum(h):
        text_out(f, bounds, hq.at[h], sc, pc, gT, t32, kv32, gt.at[h])
        for c in text_x(h):
            c.start()

    def round_own(h):
        dk[h, FT : ROWS - FT] = (acc_k[h, 2 * FT : ROWS] * SCALE).astype(BF16)
        dv[h, FT : ROWS - FT] = acc_v[h, 2 * FT : ROWS].astype(BF16)

    text_second(0)
    text_second(1)
    text_third(0)
    halo_start(0)
    text_third(1)
    halo_start(1)
    compute(0)
    halo_start(2)
    halo_back(0)
    give(0, 0)
    text_sum(0)
    round_own(0)
    add_edges(0)
    give(0, 1)
    give(0, 2)
    compute(1)
    halo_back(1)
    give(1, 0)
    text_sum(1)
    round_own(1)
    text_mid(0)
    add_edges(1)
    give(1, 1)
    give(1, 2)
    compute(2)
    halo_back(2)
    text_sum(2)
    give(2, 0)
    text_mid(1)
    round_own(2)
    add_edges(2)
    text_mid(2)
    give(2, 1)
    give(2, 2)
    for h in range(HEADS):
        for c in text_z(h):
            c.wait_recv()
        last = s1[h, slot(z)].astype(F32)
        for d in range(1, NZ):
            last = last + rz[h, d - 1].astype(F32)
        cols = slice(h * HD, (h + 1) * HD)
        for s in range(NSEG):
            ogk[s, :, cols] = last[2 * s : 2 * s + 2]
            ogv[s, :, cols] = last[8 + 2 * s : 8 + 2 * s + 2]
    for g in range(2):
        for c in text_far(g) + text_near(g) + text_over(g):
            c.wait_send()
    for h in range(HEADS):
        for c in halo_in(h) + halo_out(h) + text_x(h) + text_z(h):
            c.wait_send()
        for i in range(3):
            for c in arrivals(h, i)[1]:
                c.wait_send()
            local, moves = returns(h, i)
            local.wait()
            for c in moves:
                c.wait()


def deliver(a, b, c, d, e, oa, ob, oc, od, oe, buf, come, go):
    rows = TOK // CHUNKS
    ins, outs = [], []
    for i, (src, dst) in enumerate(((a, oa), (b, ob), (c, oc))):
        for j in range(CHUNKS):
            part = pl.ds(j * rows, rows)
            ins.append(pltpu.make_async_copy(src.at[part], buf.at[i, part], come.at[i, j]))
            outs.append(pltpu.make_async_copy(buf.at[i, part], dst.at[part], go.at[i, j]))
    for m in ins:
        m.start()
    od[...] = d[...]
    oe[...] = e[...]
    for m, n in zip(ins, outs):
        m.wait()
        n.start()
    for n in outs:
        n.wait()


def body(queries, keys, values, text_k, text_v, text_len, seg_frames):
    hbm = pl.BlockSpec(memory_space=pl.ANY)
    vmem = pl.BlockSpec(memory_space=pltpu.VMEM)
    smem = pl.BlockSpec(memory_space=pltpu.SMEM)
    dma = pltpu.SemaphoreType.DMA
    S = jax.ShapeDtypeStruct
    V = pltpu.VMEM
    H = HEADS
    shapes = (S((TOK, NU * W), BF16),) * 3 + (S((NSEG, 2, W), F32),) * 2
    grads = pl.pallas_call(
        fused,
        out_shape=shapes,
        in_specs=[smem, smem, hbm, hbm, hbm, vmem, vmem],
        out_specs=(hbm, hbm, hbm, vmem, vmem),
        scratch_shapes=[
            V((16, W), F32), V((H, 16, HD), BF16),
            V((H, ROWS, HD), BF16), V((H, EXT, HD), BF16), V((H, EXT, HD), BF16),
            V((H, NF, 16, HD), BF16), V((NF * 16, HD), F32), V((2, NSEG, TXT, HD), F32),
            V((H, 2, NSEG, TXT, HD), BF16), V((H, 2, NSEG, HD, TXT), BF16),
            V((HD, EXT), BF16), V((HD, EXT), BF16),
            V((H, EXT, HD), F32), V((H, EXT, HD), F32),
            V((TXT, ROWS), BF16), V((TXT, ROWS), BF16), V((HD, ROWS), BF16),
            V((H, ROWS, HD), BF16), V((H, ROWS, HD), BF16), V((H, ROWS, HD), BF16),
            V((H, 4, FT, HD), BF16), V((H, 4, FT, HD), BF16),
            V((H, NF, 16, HD), BF16), V((H, NX - 1, NZ, 16, HD), BF16), V((H, NZ, 16, HD), BF16),
            V((H, NZ - 1, 16, HD), BF16),
            dma((H, 3, NU)), dma((H, 3, NU)), dma((H, 4)), dma((H, 2, 2)), dma((H, 2, 2)),
            dma((2, 6)), dma((2, 6)), dma((2, NX)), dma((2, NX)),
            dma((H, 3, NU)), dma((H, 3, NU)), dma((H, 3)), dma((H, 4)), dma((H, 4)),
            dma((H, NZ)), dma((H, NZ)), dma((H, NX)), dma((H, NX)),
            pltpu.SemaphoreType.REGULAR,
        ],
        compiler_params=pltpu.CompilerParams(collective_id=0, has_side_effects=True, vmem_limit_bytes=VMEM_LIMIT),
        name="windowed_attention",
    )(text_len, seg_frames, queries, keys, values, text_k, text_v)
    return pl.pallas_call(
        deliver,
        out_shape=shapes,
        in_specs=[hbm, hbm, hbm, vmem, vmem],
        out_specs=(hbm, hbm, hbm, vmem, vmem),
        scratch_shapes=[V((3, TOK, NU * W), BF16), dma((3, CHUNKS)), dma((3, CHUNKS))],
        name="deliver",
    )(*grads)


def solution(mesh):
    rows = P(("frame", "uly"), None)
    text = P(None, "frame", "uly")
    return jax.shard_map(
        body,
        mesh=mesh,
        in_specs=(rows, rows, rows, text, text, P(), P()),
        out_specs=(rows, rows, rows, text, text),
        check_vma=False,
    )
```

```python
import math

import jax
import jax.numpy as jnp
from jax import lax
from jax.experimental import pallas as pl
from jax.experimental.pallas import tpu as pltpu
from jax.sharding import PartitionSpec as P

HD = 128
FT = 64
NSEG = 4
TXT = 128
NU = 8
NX = 4
NZ = 16
NF = NX * NZ
HEADS = 3
W = HEADS * HD
TOK = 128
ROWS = NU * TOK
EXT = ROWS + 2 * FT
TILES = EXT // TOK
SCALE = HD ** -0.5
EXP2 = SCALE * math.log2(math.e)
QUAD = 4
FAR = (4, 12, 8)
NEAR = (1, 15, 2)
MESH = pl.DeviceIdType.MESH
VMEM_LIMIT = 56 * 1024 * 1024
FAR_FIRST = (4, 3, 5, 2, 6, 1, 7)
GROUPS = (pl.ds(0, 1), pl.ds(1, 2))
CHUNKS = 2
BF16 = jnp.bfloat16
F32 = jnp.float32


def place():
    f = lax.axis_index("frame")
    u = lax.axis_index("uly")
    return f, u, lax.div(f, NZ), lax.rem(f, NZ)


def slot(z):
    return lax.rem(z, QUAD) * QUAD + lax.div(z, QUAD)


def uly_peer(f, u, d):
    return (f, lax.rem(u + d, NU))


def z_peer(x, z, u, d):
    return (x * NZ + lax.rem(z + d, NZ), u)


def x_peer(f, u, d):
    return (lax.rem(f + NZ * d, NF), u)


def greet(sem, peer):
    pl.semaphore_signal(sem, inc=1, device_id=peer, device_id_type=MESH)


def each(first, last, act):
    def one(i, carry):
        act(i)
        return carry

    lax.fori_loop(first, last, one, 0)


def meet(f, u, x, z, ready):
    barrier = pltpu.get_barrier_semaphore()
    for d in range(1, NU):
        greet(barrier, uly_peer(f, u, d))
    each(z + 1, NZ, lambda i: greet(barrier, (x * NZ + i, u)))
    each(x + 1, NX, lambda i: greet(barrier, (i * NZ + z, u)))

    @pl.when(z == 0)
    def _():
        greet(barrier, (lax.rem(f + NF - 1, NF), u))

    pl.semaphore_wait(barrier, NU - 1 + z + x + (z == NZ - 1).astype(jnp.int32))
    each(0, z, lambda i: greet(ready, (x * NZ + i, u)))
    each(0, x, lambda i: greet(ready, (i * NZ + z, u)))

    @pl.when(z == NZ - 1)
    def _():
        greet(ready, (lax.rem(f + 1, NF), u))


def remote(src, dst, send, recv, peer):
    return pltpu.make_async_remote_copy(
        src_ref=src, dst_ref=dst, send_sem=send, recv_sem=recv, device_id=peer, device_id_type=MESH
    )


def dot(a, b, ca, cb):
    return lax.dot_general(a, b, (((ca,), (cb,)), ((), ())), preferred_element_type=F32)


def softmax(scores):
    top = jnp.max(scores, axis=0, keepdims=True)
    e = jnp.exp2((scores - top) * EXP2)
    return e * (1.0 / jnp.sum(e, axis=0, keepdims=True))


def bounds_of(segs):
    b0 = segs[0]
    b1 = b0 + segs[1]
    b2 = b1 + segs[2]
    return b0, b1, b2


def segment(frame, bounds):
    return sum((frame >= b).astype(jnp.int32) for b in bounds)


def text_in(tg, t32, kv32, tkv, tkvT):
    t32[...] = tg[...].reshape(NF * 16, HD).astype(F32)
    for c in range(2):
        for s in range(NSEG):
            for t in range(2):
                kv32[c, s, pl.ds(t, NF, stride=2), :] = t32[pl.ds(c * 8 + s * 2 + t, NF, stride=16), :]
            part = kv32[c, s]
            tkv[c, s] = part.astype(BF16)
            tkvT[c, s] = part.T.astype(BF16)


def turn(src, dst, tiles):
    for t in tiles:
        dst[:, t * TOK : (t + 1) * TOK] = src[t * TOK : (t + 1) * TOK, :].T


def halves(left, c):
    none = jnp.zeros_like(c)
    return jnp.concatenate([jnp.where(left, c, none), jnp.where(left, none, c)], axis=0)


def pairs_step(pairs, f, lens, bounds, hq, hk, hv, kT, vT, tkv, tkvT, dq, acc_k, acc_v, sc, pc, gT):
    row = lax.broadcasted_iota(jnp.int32, (4 * FT, 2 * FT), 0)
    lane = lax.broadcasted_iota(jnp.int32, (4 * FT, 2 * FT), 1)
    place_of = lax.broadcasted_iota(jnp.int32, (TXT, 2 * FT), 0)
    trow = (place_of & 97) | ((place_of & 6) << 2) | ((place_of & 24) >> 2)
    left = lax.broadcasted_iota(jnp.int32, (TXT, 2 * FT), 1) < FT
    work = []
    for p in pairs:
        low = jnp.logical_and(f == 0, p == 0).astype(jnp.int32)
        high = jnp.logical_and(f == NF - 1, p == ROWS // TOK - 1).astype(jnp.int32)
        bad = ((row < FT) & (lane >= FT * (1 - low))) | ((row >= 3 * FT) & (lane < FT * (1 + high)))
        qr = pl.ds(pl.multiple_of(p * TOK, TOK), TOK)
        kr = pl.ds(pl.multiple_of(p * TOK, TOK), 4 * FT)
        s0 = segment(f * (ROWS // FT) + 2 * p, bounds)
        s1 = segment(f * (ROWS // FT) + 2 * p + 1, bounds)
        n = jnp.where(left, lens[s0], lens[s1])
        work.append((bad, qr, kr, s0, s1, n))
    qs = [hq[w[1], :] for w in work]
    ks = [hk[w[2], :] for w in work]
    vs = [hv[w[2], :] for w in work]
    ss = [dot(k, q, 1, 1) for k, q in zip(ks, qs)]
    cs = [
        jnp.where(left, dot(tkv[0, w[3]], q, 1, 1), dot(tkv[0, w[4]], q, 1, 1)) for w, q in zip(work, qs)
    ]
    ps = [softmax(jnp.where(w[0], -1e30, s)) for w, s in zip(work, ss)]
    cps = [softmax(jnp.where(trow < w[5], c, -1e30)) for w, c in zip(work, cs)]
    p16 = [p.astype(BF16) for p in ps]
    cp16 = [c.astype(BF16) for c in cps]
    so = [dot(vT[:, w[2]], p, 1, 0) for w, p in zip(work, p16)]
    co = [
        dot(jnp.concatenate([tkvT[1, w[3]], tkvT[1, w[4]]], axis=1), halves(left, c), 1, 0) for w, c in zip(work, cp16)
    ]
    g16 = [(a + b).astype(BF16) for a, b in zip(so, co)]
    sd = [jnp.sum(g.astype(F32) * a, axis=0, keepdims=True) for g, a in zip(g16, so)]
    cd = [jnp.sum(g.astype(F32) * a, axis=0, keepdims=True) for g, a in zip(g16, co)]
    ds = [(p * (dot(v, g, 1, 0) - d)).astype(BF16) for p, v, g, d in zip(ps, vs, g16, sd)]
    dcs = [
        (c * (jnp.where(left, dot(tkv[1, w[3]], g, 1, 0), dot(tkv[1, w[4]], g, 1, 0)) - d)).astype(BF16)
        for c, w, g, d in zip(cps, work, g16, cd)
    ]
    dqs = [
        dot(
            jnp.concatenate([kT[:, w[2]], tkvT[0, w[3]], tkvT[0, w[4]]], axis=1),
            jnp.concatenate([s, halves(left, c)], axis=0), 1, 0,
        )
        for w, s, c in zip(work, ds, dcs)
    ]
    dks = [acc_k[w[2], :] + dot(s, q, 1, 0) for w, s, q in zip(work, ds, qs)]
    dvs = [acc_v[w[2], :] + dot(p, g, 1, 1) for w, p, g in zip(work, p16, g16)]
    for i, w in enumerate(work):
        dq[w[1], :] = (dqs[i] * SCALE).T.astype(BF16)
        acc_k[w[2], :] = dks[i]
        acc_v[w[2], :] = dvs[i]
        sc[:, w[1]] = dcs[i]
        pc[:, w[1]] = cp16[i]
        gT[:, w[1]] = g16[i]


def text_out(f, bounds, hq, sc, pc, gT, t32, kv32, gt):
    frame = f * (ROWS // FT) + lax.broadcasted_iota(jnp.int32, (16, ROWS), 1) // FT
    seg = segment(frame, bounds)
    q = hq[...]
    g = gT[...]
    on = [jnp.broadcast_to((seg == s).astype(F32).astype(BF16)[0:1], (TXT, ROWS)) for s in range(NSEG)]
    gk = dot(jnp.concatenate([sc[...] * m for m in on], axis=0), q, 1, 0) * SCALE
    gv = dot(jnp.concatenate([pc[...] * m for m in on], axis=0), g, 1, 1)
    for s in range(NSEG):
        kv32[0, s] = gk[s * TXT : (s + 1) * TXT]
        kv32[1, s] = gv[s * TXT : (s + 1) * TXT]
    for c in range(2):
        for s in range(NSEG):
            for t in range(2):
                t32[pl.ds(c * 8 + s * 2 + t, NF, stride=16), :] = kv32[c, s, pl.ds(t, NF, stride=2), :]
    gt[...] = t32[...].astype(BF16).reshape(NF, 16, HD)


def fused(
    lens, segs, q, k, v, tk_in, tv_in, oq, ok, ov, ogk, ogv,
    slab32, slab, hq, hk, hv, tg, t32, kv32, tkv, tkvT, kT, vT, acc_k, acc_v, sc, pc, gT,
    dq, dk, dv, hsend, hrecv, gt, rx, s1, rz,
    a_send, a_recv, l_sem, h_send, h_recv, z_send, z_recv, x_send, x_recv,
    b_send, b_recv, m_sem, e_send, e_recv, w_send, w_recv, y_send, y_recv, ready,
):
    f, u, x, z = place()
    bounds = bounds_of(segs)
    after = (lax.rem(f + 1, NF), u)
    before = (lax.rem(f + NF - 1, NF), u)
    for s in range(NSEG):
        slab32[2 * s : 2 * s + 2, :] = tk_in[s].astype(F32)
        slab32[8 + 2 * s : 8 + 2 * s + 2, :] = tv_in[s].astype(F32)
    for h in range(HEADS):
        slab[h] = slab32[:, h * HD : (h + 1) * HD].astype(BF16)
    meet(f, u, x, z, ready)

    block = pl.ds(x * NZ, NZ)

    here = x * NZ + slot(z)
    row = pl.ds(x * NZ + lax.rem(z, QUAD) * QUAD, QUAD)

    def text_own(g):
        return pltpu.make_async_copy(slab.at[GROUPS[g]], tg.at[GROUPS[g], here], l_sem.at[g, 3])

    def text_far(g):
        return [
            remote(slab.at[GROUPS[g]], tg.at[GROUPS[g], here], z_send.at[g, i], z_recv.at[g, i], z_peer(x, z, u, d))
            for i, d in enumerate(FAR)
        ]

    def text_near(g):
        part = tg.at[GROUPS[g], row]
        return [
            remote(part, part, z_send.at[g, 3 + i], z_recv.at[g, 3 + i], z_peer(x, z, u, d)) for i, d in enumerate(NEAR)
        ]

    def text_over(g):
        part = tg.at[GROUPS[g], block]
        return [remote(part, part, x_send.at[g, d], x_recv.at[g, d], x_peer(f, u, d)) for d in range(1, NX)]

    def text_first(g, lower):
        for c, d in zip(text_far(g), FAR):
            pl.when((lax.rem(z + d, NZ) < z) == lower)(c.start)

    def text_second(g):
        text_own(g).wait()
        for c in text_far(g):
            c.wait_recv()
        for c in text_near(g):
            c.start()

    def text_third(g):
        for c in text_near(g):
            c.wait_recv()
        for c in text_over(g):
            c.start()

    def arrivals(h, i):
        src, dst, off = ((k, hk, FT), (v, hv, FT), (q, hq, 0))[i]
        rows = pl.ds(pl.multiple_of(off + u * TOK, FT), TOK)
        mine = pl.ds(pl.multiple_of(u * W + h * HD, HD), HD)
        local = pltpu.make_async_copy(src.at[:, mine], dst.at[h, rows], l_sem.at[h, i])
        moves = []
        for d in FAR_FIRST:
            peer = uly_peer(f, u, d)
            cols = pl.ds(pl.multiple_of(peer[1] * W + h * HD, HD), HD)
            moves.append(remote(src.at[:, cols], dst.at[h, rows], a_send.at[h, i, d], a_recv.at[h, i, d], peer))
        return local, moves

    def issue(h, i):
        local, moves = arrivals(h, i)
        local.start()
        for c in moves:
            c.start()

    def landed(h, i):
        local, moves = arrivals(h, i)
        local.wait()
        for c in moves:
            c.wait_recv()

    def halo_in(h):
        out = []
        for i, ref in enumerate((hk, hv)):
            lo, hi = ref.at[h, pl.ds(FT, FT)], ref.at[h, pl.ds(ROWS, FT)]
            out.append(remote(lo, ref.at[h, pl.ds(FT + ROWS, FT)], h_send.at[h, i, 0], h_recv.at[h, i, 0], before))
            out.append(remote(hi, ref.at[h, pl.ds(0, FT)], h_send.at[h, i, 1], h_recv.at[h, i, 1], after))
        return out

    def halo_out(h):
        out = []
        for i in range(2):
            out.append(remote(hsend.at[h, 2 * i], hrecv.at[h, 2 * i + 1], e_send.at[h, 2 * i], e_recv.at[h, 2 * i], before))
            out.append(
                remote(hsend.at[h, 2 * i + 1], hrecv.at[h, 2 * i], e_send.at[h, 2 * i + 1], e_recv.at[h, 2 * i + 1], after)
            )
        return out

    def returns(h, i):
        src, dst = ((dq, oq), (dk, ok), (dv, ov))[i]
        cols = pl.ds(pl.multiple_of(u * W + h * HD, HD), HD)
        own = pl.ds(pl.multiple_of(u * TOK, TOK), TOK)
        local = pltpu.make_async_copy(src.at[h, own], dst.at[:, cols], m_sem.at[h, i])
        moves = []
        for d in FAR_FIRST:
            peer = uly_peer(f, u, d)
            rows = pl.ds(pl.multiple_of(peer[1] * TOK, TOK), TOK)
            moves.append(remote(src.at[h, rows], dst.at[:, cols], b_send.at[h, i, d], b_recv.at[h, i, d], peer))
        return local, moves

    def text_x(h):
        out = []
        for d in range(1, NX):
            part = pl.ds(lax.rem(x + d, NX) * NZ, NZ)
            out.append(remote(gt.at[h, part], rx.at[h, d - 1], y_send.at[h, d], y_recv.at[h, d], x_peer(f, u, d)))
        return out

    def text_z(h):
        return [
            remote(s1.at[h, slot(lax.rem(z + d, NZ))], rz.at[h, d - 1], w_send.at[h, d], w_recv.at[h, d], z_peer(x, z, u, d))
            for d in range(1, NZ)
        ]

    def give(h, i):
        local, moves = returns(h, i)
        local.start()
        for c in moves:
            c.start()

    def add_edges(h):
        for c in halo_out(h):
            c.wait_recv()
        for i, (acc, out) in enumerate(((acc_k, dk), (acc_v, dv))):
            scale = SCALE if i == 0 else 1.0
            out[h, 0:FT] = (acc[h, FT : 2 * FT] * scale + hrecv[h, 2 * i].astype(F32)).astype(BF16)
            out[h, ROWS - FT : ROWS] = (acc[h, ROWS : ROWS + FT] * scale + hrecv[h, 2 * i + 1].astype(F32)).astype(BF16)

    def text_mid(h):
        for c in text_x(h):
            c.wait_recv()
        total = gt[h, block].astype(F32)
        for d in range(1, NX):
            total = total + rx[h, d - 1].astype(F32)
        s1[h] = total.astype(BF16)
        for c in text_z(h):
            c.start()

    for g in range(2):
        text_own(g).start()
        text_first(g, True)
    for h in range(HEADS):
        for i in range(3):
            issue(h, i)
    later = NZ - 1 - z + NX - 1 - x + (z == 0).astype(jnp.int32)

    @pl.when(later > 0)
    def _():
        pl.semaphore_wait(ready, later)

    for g in range(2):
        text_first(g, False)
    acc_k[...] = jnp.zeros_like(acc_k)
    acc_v[...] = jnp.zeros_like(acc_v)

    def halo_start(h):
        landed(h, 0)
        landed(h, 1)
        for c in halo_in(h):
            c.start()

    def compute(h):
        turn(hk.at[h], kT, range(1, TILES - 1))
        turn(hv.at[h], vT, range(1, TILES - 1))
        if h < 2:
            for c in text_over(h):
                c.wait_recv()
        text_in(tg.at[h], t32, kv32, tkv.at[h], tkvT.at[h])
        landed(h, 2)
        refs = (
            f, lens, bounds, hq.at[h], hk.at[h], hv.at[h], kT, vT, tkv.at[h], tkvT.at[h], dq.at[h],
            acc_k.at[h], acc_v.at[h], sc, pc, gT,
        )

        def inner(i, carry):
            pairs_step((i + 1, i + 4), *refs)
            return carry

        lax.fori_loop(0, 3, inner, 0)
        for c in halo_in(h):
            c.wait_recv()
        turn(hk.at[h], kT, (0, TILES - 1))
        turn(hv.at[h], vT, (0, TILES - 1))
        pairs_step((0, 7), *refs)

    def halo_back(h):
        for i, acc in enumerate((acc_k, acc_v)):
            scale = SCALE if i == 0 else 1.0
            hsend[h, 2 * i] = (acc[h, 0:FT] * scale).astype(BF16)
            hsend[h, 2 * i + 1] = (acc[h, FT + ROWS : EXT] * scale).astype(BF16)
        for c in halo_out(h):
            c.start()

    def text_sum(h):
        text_out(f, bounds, hq.at[h], sc, pc, gT, t32, kv32, gt.at[h])
        for c in text_x(h):
            c.start()

    def round_own(h):
        dk[h, FT : ROWS - FT] = (acc_k[h, 2 * FT : ROWS] * SCALE).astype(BF16)
        dv[h, FT : ROWS - FT] = acc_v[h, 2 * FT : ROWS].astype(BF16)

    text_second(0)
    text_second(1)
    text_third(0)
    halo_start(0)
    text_third(1)
    halo_start(1)
    compute(0)
    halo_start(2)
    halo_back(0)
    give(0, 0)
    text_sum(0)
    round_own(0)
    add_edges(0)
    give(0, 1)
    give(0, 2)
    compute(1)
    halo_back(1)
    give(1, 0)
    text_sum(1)
    round_own(1)
    text_mid(0)
    add_edges(1)
    give(1, 1)
    give(1, 2)
    compute(2)
    halo_back(2)
    text_sum(2)
    give(2, 0)
    text_mid(1)
    round_own(2)
    add_edges(2)
    text_mid(2)
    give(2, 1)
    give(2, 2)
    for h in range(HEADS):
        for c in text_z(h):
            c.wait_recv()
        last = s1[h, slot(z)].astype(F32)
        for d in range(1, NZ):
            last = last + rz[h, d - 1].astype(F32)
        cols = slice(h * HD, (h + 1) * HD)
        for s in range(NSEG):
            ogk[s, :, cols] = last[2 * s : 2 * s + 2]
            ogv[s, :, cols] = last[8 + 2 * s : 8 + 2 * s + 2]
    for g in range(2):
        for c in text_far(g) + text_near(g) + text_over(g):
            c.wait_send()
    for h in range(HEADS):
        for c in halo_in(h) + halo_out(h) + text_x(h) + text_z(h):
            c.wait_send()
        for i in range(3):
            for c in arrivals(h, i)[1]:
                c.wait_send()
            local, moves = returns(h, i)
            local.wait()
            for c in moves:
                c.wait()


def deliver(a, b, c, d, e, oa, ob, oc, od, oe, buf, tbuf, come, go):
    rows = TOK // CHUNKS
    ins, outs = [], []
    for j in range(CHUNKS):
        for i, (src, dst) in enumerate(((a, oa), (b, ob), (c, oc))):
            part = pl.ds(j * rows, rows)
            ins.append(pltpu.make_async_copy(src.at[part], buf.at[i, part], come.at[i, j]))
            outs.append(pltpu.make_async_copy(buf.at[i, part], dst.at[part], go.at[i, j]))
    for i, (src, dst) in enumerate(((d, od), (e, oe))):
        ins.append(pltpu.make_async_copy(src, tbuf.at[i], come.at[3, i]))
        outs.append(pltpu.make_async_copy(tbuf.at[i], dst, go.at[3, i]))
    for m in ins:
        m.start()
    for m, n in zip(ins, outs):
        m.wait()
        n.start()
    for n in outs:
        n.wait()


def body(queries, keys, values, text_k, text_v, text_len, seg_frames):
    hbm = pl.BlockSpec(memory_space=pl.ANY)
    vmem = pl.BlockSpec(memory_space=pltpu.VMEM)
    smem = pl.BlockSpec(memory_space=pltpu.SMEM)
    dma = pltpu.SemaphoreType.DMA
    S = jax.ShapeDtypeStruct
    V = pltpu.VMEM
    H = HEADS
    shapes = (S((TOK, NU * W), BF16),) * 3 + (S((NSEG, 2, W), F32),) * 2
    grads = pl.pallas_call(
        fused,
        out_shape=shapes,
        in_specs=[smem, smem, hbm, hbm, hbm, vmem, vmem],
        out_specs=(hbm, hbm, hbm, vmem, vmem),
        scratch_shapes=[
            V((16, W), F32), V((H, 16, HD), BF16),
            V((H, ROWS, HD), BF16), V((H, EXT, HD), BF16), V((H, EXT, HD), BF16),
            V((H, NF, 16, HD), BF16), V((NF * 16, HD), F32), V((2, NSEG, TXT, HD), F32),
            V((H, 2, NSEG, TXT, HD), BF16), V((H, 2, NSEG, HD, TXT), BF16),
            V((HD, EXT), BF16), V((HD, EXT), BF16),
            V((H, EXT, HD), F32), V((H, EXT, HD), F32),
            V((TXT, ROWS), BF16), V((TXT, ROWS), BF16), V((HD, ROWS), BF16),
            V((H, ROWS, HD), BF16), V((H, ROWS, HD), BF16), V((H, ROWS, HD), BF16),
            V((H, 4, FT, HD), BF16), V((H, 4, FT, HD), BF16),
            V((H, NF, 16, HD), BF16), V((H, NX - 1, NZ, 16, HD), BF16), V((H, NZ, 16, HD), BF16),
            V((H, NZ - 1, 16, HD), BF16),
            dma((H, 3, NU)), dma((H, 3, NU)), dma((H, 4)), dma((H, 2, 2)), dma((H, 2, 2)),
            dma((2, 6)), dma((2, 6)), dma((2, NX)), dma((2, NX)),
            dma((H, 3, NU)), dma((H, 3, NU)), dma((H, 3)), dma((H, 4)), dma((H, 4)),
            dma((H, NZ)), dma((H, NZ)), dma((H, NX)), dma((H, NX)),
            pltpu.SemaphoreType.REGULAR,
        ],
        compiler_params=pltpu.CompilerParams(collective_id=0, has_side_effects=True, vmem_limit_bytes=VMEM_LIMIT),
        name="windowed_attention",
    )(text_len, seg_frames, queries, keys, values, text_k, text_v)
    return pl.pallas_call(
        deliver,
        out_shape=shapes,
        in_specs=[hbm] * 5,
        out_specs=(hbm,) * 5,
        scratch_shapes=[V((3, TOK, NU * W), BF16), V((2, NSEG, 2, W), F32), dma((4, CHUNKS)), dma((4, CHUNKS))],
        compiler_params=pltpu.CompilerParams(vmem_limit_bytes=8 * 1024 * 1024),
        name="deliver",
    )(*grads)


def solution(mesh):
    rows = P(("frame", "uly"), None)
    text = P(None, "frame", "uly")
    return jax.shard_map(
        body,
        mesh=mesh,
        in_specs=(rows, rows, rows, text, text, P(), P()),
        out_specs=(rows, rows, rows, text, text),
        check_vma=False,
    )
```
